128 devices in a mesh: attn: 4 (over x_lo, core), expert: 32 (over z, y, x_hi).
Axes of the slice: x: 4 (x_hi: 2, x_lo: 2; x = x_hi * 2 + x_lo), y: 4, z: 4, core: 2. Of those that a mesh axis runs over, the one named last changes fastest.
Arguments:
- tokens: bfloat16 [1024, 7168], P(('attn', 'expert')), may hold values from -6 to 6
- gates: float32 [1024, 8], P(('attn', 'expert')), may hold values from 0.1 to 1
- top_ids: int32 [1024, 8], P(('attn', 'expert')), may hold values from 0 to 31, all different within a row; in each aligned block of 8 rows (0 to 7, 8 to 15, ...) at most 3 rows name the same one
- home_expert: int32 [32], replicated, may hold values from 0 to 31, each once
- copy_source: int32 [32], replicated, may hold values from 0 to 31
- home_gate: bfloat16 [32, 7168, 1024], P('expert', None, 'attn'), may hold values from -0.0625 to 0.0625
- home_up: bfloat16 [32, 7168, 1024], P('expert', None, 'attn'), may hold values from -0.0625 to 0.0625
- home_down: bfloat16 [32, 7168, 1024], P('expert', None, 'attn'), may hold values from -0.1875 to 0.1875
Outputs:
- mixed: bfloat16 [1024, 7168], P(('attn', 'expert'))
- replica_gate: bfloat16 [32, 7168, 1024], P('expert', None, 'attn')
- replica_up: bfloat16 [32, 7168, 1024], P('expert', None, 'attn')
- replica_down: bfloat16 [32, 7168, 1024], P('expert', None, 'attn')
The draws below stay inside these ranges and needn't reach their ends.
Inputs may be any that keep to these rules, and one draw needn't show every extreme that they name: `top_ids`: among the 8 rows of one device no expert is named by more than 3 rows, a bound that some block reaches.
All inputs are finite; a program needn't handle non-finite values.
Results may differ from the reference program's by a relative error of at most 0.015.
Values may be sent and summed in bfloat16 or wider, within the bound.
No kernel may reach another device: no remote copies, remote signals or barrier semaphores. Data moves between devices by JAX's collectives and lax.ppermute only.
A program may use at most 128 MiB of HBM per device.

```python
import math
import jax
import jax.numpy as jnp
import numpy as np
from jax import lax

D = 7168
FF = 1024
TOPK = 8
TOK_DEV = 8
EXPERTS = 32
TOKENS = 1024
MOST = 3
N_ATTN = 4


def place_ends(array, own_key, smallest, high):
    spot = [jax.random.randint(jax.random.fold_in(own_key, axis), (), 0, length) for axis, length in enumerate(array.shape)]
    widest = array.shape.index(max(array.shape))
    next_to = spot[:widest] + [(spot[widest] + 1) % array.shape[widest]] + spot[widest + 1:]
    return array.at[tuple(spot)].set(smallest).at[tuple(next_to)].set(high)


def shard_levels(own_key, dims, pieces, smallest, top_value):
    def one(axis_at, shards_of):
        heights = jax.random.uniform(jax.random.fold_in(jax.random.fold_in(own_key, 6), axis_at), (shards_of,), jnp.float32, smallest / len(pieces), top_value / len(pieces))
        return jnp.repeat(jnp.exp(heights), dims[axis_at] // shards_of).reshape((-1,) + (1,) * (len(dims) - axis_at - 1))

    factor_of = one(*pieces[0])
    for cut in pieces[1:]:
        factor_of = factor_of * one(*cut)
    return factor_of


def assign_block(rng, own, number, rows, amount, top, reach, slope):
    order = jax.random.permutation(rng, amount)
    heavy_load, usual = load_shares(amount, rows * top, reach, slope, True), load_shares(amount, rows * top, reach, slope, False)
    places = jnp.arange(amount)

    def named(lengths, rotation):
        used = int((lengths > 0).sum())
        fixed = max(1, used // 4)
        moved = fixed + (places - fixed + rotation * (used - fixed)) % max(1, amount - fixed)
        return jnp.zeros((amount,), jnp.int32).at[order[jnp.where(places < fixed, places, moved)]].set(jnp.asarray(lengths, jnp.int32))

    lengths = jnp.where(number % 4 == 0, named(heavy_load, number // 4), named(usual, number - number // 4 - 1))
    mixed = jax.random.permutation(jax.random.fold_in(own, 3), amount)
    source_of, sink = mixed[0:amount // 2 * 2:2], mixed[1:amount // 2 * 2:2]
    slack = jnp.minimum(lengths[source_of] - 1, reach - lengths[sink]) // 2
    slack = jnp.where((source_of == order[0]) | (sink == order[0]) | (lengths[sink] == 0), 0, jnp.maximum(slack, 0))
    moved = jax.random.randint(jax.random.fold_in(own, 4), (amount // 2,), 0, 1 << 20) % (slack + 1)
    lengths = lengths.at[source_of].add(-moved).at[sink].add(moved)
    labels = jnp.searchsorted(jnp.cumsum(lengths), jnp.arange(rows * top), side="right").astype(jnp.int32)
    grid = labels.reshape(top, rows).T
    grid = grid[jax.random.permutation(jax.random.fold_in(own, 1), rows)]
    rotation = jax.random.randint(jax.random.fold_in(own, 2), (rows, 1), 0, top)
    return jnp.take_along_axis(grid, (jnp.arange(top)[None, :] + rotation) % top, axis=1)


def load_shares(amount, total, most, skew, full):
    loads = [(1 << 20) // math.isqrt(standing ** skew) + 1 for standing in range(1, amount + 1)]
    largest = most if full else min(most, max(-(-total // amount), total * loads[0] // sum(loads)))
    least = 1 if total - largest >= amount - 1 else 0
    holding, spare = [largest] + [least] * (amount - 1), total - largest - least * (amount - 1)
    while spare > 0:
        free = [i for i in range(1, amount) if holding[i] < largest] or [i for i in range(1, amount) if holding[i] < most]
        pool, left = sum([loads[i] for i in free]), spare
        for i in free:
            more = min(most - holding[i], max(1, left * loads[i] // pool), spare)
            holding[i] = holding[i] + more
            spare = spare - more
    return np.array(holding)


def normal_values(key, extent, scale, most, shards=(), kind=jnp.bfloat16):
    gain = shard_levels(key, extent, shards, -0.22, 0.18) if shards else 1.0
    entries = jax.random.normal(key, extent, jnp.float32) * scale * gain
    return jnp.minimum(jnp.maximum(entries, -most), most).astype(kind)


def setup_inputs(seed: int = 0) -> dict:
    streams_of = jax.random.split(jax.random.key(seed), 9)
    tokens = normal_values(streams_of[0], (TOKENS, D), 1.0, 6.0, ((0, 128),))
    gates = jnp.clip(0.1 + 0.9 * jax.random.uniform(streams_of[1], (TOKENS, TOPK), jnp.float32) ** shard_levels(streams_of[1], (TOKENS, TOPK), ((0, 128),), -0.2, 0.2), 0.1, 1.0)
    top_ids_keys = jax.random.split(jax.random.fold_in(streams_of[2], 1), TOKENS // TOK_DEV)
    top_ids_turns = jax.random.permutation(jax.random.fold_in(streams_of[2], 3), TOKENS // TOK_DEV)
    top_ids = jax.vmap(lambda own, number: assign_block(jax.random.fold_in(streams_of[2], 2), own, number, TOK_DEV, EXPERTS, TOPK, MOST, 2))(top_ids_keys, top_ids_turns).reshape((TOKENS, TOPK))
    home_expert = jax.random.permutation(streams_of[3], EXPERTS).astype(jnp.int32)
    copy_source = place_ends(jax.random.randint(streams_of[4], (EXPERTS,), 0, EXPERTS), jax.random.fold_in(streams_of[4], 1), 0, EXPERTS - 1).astype(jnp.int32)
    home_gate = normal_values(streams_of[5], (EXPERTS, D, FF), D ** -0.5, 0.0625, ((0, 32), (2, 4)))
    home_up = normal_values(streams_of[6], (EXPERTS, D, FF), D ** -0.5, 0.0625, ((0, 32), (2, 4)))
    home_down = normal_values(streams_of[7], (EXPERTS, D, FF), FF ** -0.5, 0.1875, ((0, 32), (2, 4)))
    return {"tokens": tokens, "gates": gates, "top_ids": top_ids, "home_expert": home_expert, "copy_source": copy_source, "home_gate": home_gate, "home_up": home_up, "home_down": home_down}


def reference(tokens, gates, top_ids, home_expert, copy_source, home_gate, home_up, home_down):
    holder_ids = jnp.arange(EXPERTS, dtype=jnp.int32)
    quarter = FF // N_ATTN

    def one_expert(mixed_sum, expert_id):
        holder = jnp.sum(jnp.where(home_expert == expert_id, holder_ids, 0)).astype(jnp.int32)
        w_gate = lax.dynamic_index_in_dim(home_gate, holder, 0, keepdims=False)
        w_up = lax.dynamic_index_in_dim(home_up, holder, 0, keepdims=False)
        w_down = lax.dynamic_index_in_dim(home_down, holder, 0, keepdims=False)
        gate_act = jnp.dot(tokens, w_gate, preferred_element_type=jnp.float32)
        up_act = jnp.dot(tokens, w_up, preferred_element_type=jnp.float32)
        hidden = (jax.nn.silu(gate_act) * up_act).astype(jnp.bfloat16)
        expert_out = jnp.zeros((TOKENS, D), jnp.float32)
        for quarter_index in range(N_ATTN):
            lower = quarter_index * quarter
            down_part = lax.dot_general(hidden[:, lower:lower + quarter], w_down[:, lower:lower + quarter],
                                        (((1,), (1,)), ((), ())), preferred_element_type=jnp.float32)
            rounded = lax.optimization_barrier(down_part.astype(jnp.bfloat16))
            expert_out = expert_out + rounded.astype(jnp.float32)
        expert_out = lax.optimization_barrier(expert_out.astype(jnp.bfloat16)).astype(jnp.float32)
        weight = jnp.sum(jnp.where(top_ids == expert_id, gates, jnp.zeros_like(gates)), axis=1)
        return mixed_sum + weight[:, None] * expert_out, None

    mixed_sum, unused = lax.scan(one_expert, jnp.zeros((TOKENS, D), jnp.float32), holder_ids)
    return (mixed_sum.astype(jnp.bfloat16), home_gate[copy_source], home_up[copy_source], home_down[copy_source])
```

```python
import jax
import jax.numpy as jnp
from jax import lax
from jax.sharding import PartitionSpec as P

LANES = 128
CORE_SWAP = [(0, 1), (1, 0), (2, 3), (3, 2)]
CHIP_SWAP = [(0, 2), (1, 3), (2, 0), (3, 1)]


def swap_blocks(blocks):
    return lax.all_to_all(blocks, "expert", split_axis=0, concat_axis=0, tiled=True)


def on_device(tokens, gates, top_ids, home_expert, copy_source, home_gate, home_up, home_down):
    experts = lax.axis_size("expert")
    rows, width = tokens.shape
    fanout = top_ids.shape[1]
    pairs = rows * fanout
    capacity = min(rows, (pairs + experts - 1) // experts + 1)
    places = experts * capacity
    slabs = width // LANES
    depth, units = home_gate.shape[1:]
    share = depth // experts

    named = top_ids.reshape(pairs)[:, None] == home_expert[None, :]
    onehot = named.astype(jnp.int32)
    rank = jnp.sum(onehot * (jnp.cumsum(onehot, axis=0) - onehot), axis=1)
    slot = jnp.sum(onehot * jnp.arange(experts, dtype=jnp.int32)[None, :], axis=1)
    target = slot * capacity + rank
    landing = target[None, :] == jnp.arange(places, dtype=jnp.int32)[:, None]
    row_of = jnp.arange(pairs, dtype=jnp.int32) // fanout
    taken = jnp.sum(jnp.where(landing, row_of[None, :], 0), axis=1)

    weights = (home_gate, home_up, home_down)
    spread = [swap_blocks(w.reshape(experts, share, units)) for w in weights]
    replicas = [swap_blocks(s[copy_source]).reshape(1, depth, units) for s in spread]

    outbound = tokens.reshape(rows, slabs, LANES)[taken]
    arrived = swap_blocks(outbound.reshape(experts, capacity * slabs, LANES))
    arrived = arrived.reshape(places, slabs, LANES)
    both = jnp.concatenate([arrived, lax.ppermute(arrived, "attn", CHIP_SWAP)], axis=0)
    slot_rows = jnp.concatenate([both, lax.ppermute(both, "attn", CORE_SWAP)], axis=0)
    slot_rows = slot_rows.reshape(4 * places, width)

    gate_act = jnp.dot(slot_rows, home_gate[0], preferred_element_type=jnp.float32)
    up_act = jnp.dot(slot_rows, home_up[0], preferred_element_type=jnp.float32)
    hidden = (jax.nn.silu(gate_act) * up_act).astype(jnp.bfloat16)
    partial = lax.dot_general(
        hidden, home_down[0], (((1,), (1,)), ((), ())), preferred_element_type=jnp.float32
    ).astype(jnp.bfloat16)

    kept, sent = partial[: 2 * places], partial[2 * places :]
    pair_sum = kept.astype(jnp.float32) + lax.ppermute(sent, "attn", CORE_SWAP).astype(jnp.float32)
    far = lax.ppermute(pair_sum[places:].astype(jnp.bfloat16), "attn", CHIP_SWAP)
    expert_out = (pair_sum[:places] + far.astype(jnp.float32)).astype(jnp.bfloat16)

    answered = swap_blocks(expert_out.reshape(experts, capacity * slabs, LANES))
    answered = answered.reshape(places, width)
    mixing = jnp.sum(
        jnp.where(landing, gates.reshape(pairs)[None, :], 0.0).reshape(places, rows, fanout), axis=2
    )
    mixed = lax.dot_general(
        mixing,
        answered.astype(jnp.float32),
        (((0,), (0,)), ((), ())),
        precision=lax.Precision.HIGHEST,
        preferred_element_type=jnp.float32,
    ).astype(jnp.bfloat16)
    return (mixed, *replicas)


def solution(mesh):
    row_spec = P(("attn", "expert"), None)
    weight_spec = P("expert", None, "attn")
    return jax.shard_map(
        on_device,
        mesh=mesh,
        in_specs=(row_spec, row_spec, row_spec, P(), P(), weight_spec, weight_spec, weight_spec),
        out_specs=(row_spec, weight_spec, weight_spec, weight_spec),
        check_vma=False,
    )
```

```python
import functools

import jax
import jax.numpy as jnp
from jax import lax
from jax.experimental import pallas as pl
from jax.experimental.pallas import tpu as pltpu
from jax.sharding import PartitionSpec as P

RING = 4
NOTE = 128
EXPERT_AXIS = RING * RING * 2
WORK = 1 << 36
BOTH = ("attn", "expert")


def table(step):
    pairs = []
    for x_lo in range(2):
        for core in range(2):
            for z in range(RING):
                for y in range(RING):
                    for x_hi in range(2):
                        to = step(x_lo, core, z, y, x_hi)
                        ends = []
                        for a, c, k, j, i in ((x_lo, core, z, y, x_hi), to):
                            slot = ((k % RING) * RING + j % RING) * 2 + i % 2
                            ends.append(((a % 2) * 2 + c % 2) * EXPERT_AXIS + slot)
                        pairs.append(tuple(ends))
    return pairs


def row_step(n):
    return table(lambda a, c, z, y, x: (a + n % 2, c, z, y, x + n // 2))


def wide_step(n):
    return table(lambda a, c, z, y, x: (a, c, z + n * c, y + n * (1 - c), x))


def deep_step(n):
    return table(lambda a, c, z, y, x: (a, c, z + n * (1 - c), y + n * c, x))


CORE_SWAP = table(lambda a, c, z, y, x: (a, c + 1, z, y, x))


def send(value, pairs):
    return lax.ppermute(value, BOTH, pairs)


def swap_blocks(blocks):
    return lax.all_to_all(blocks, "expert", split_axis=0, concat_axis=0, tiled=True)


def bf16_pieces(values):
    pieces, rest = [], values
    for _ in range(3):
        piece = lax.reduce_precision(rest, exponent_bits=8, mantissa_bits=7)
        pieces.append(piece.astype(jnp.bfloat16))
        rest = rest - piece
    return pieces


def select_kernel(fanout, capacity, chunk, column_ref, *refs):
    blocks, (chosen_ref, mixing_ref) = refs[:RING], refs[RING:]
    width = chosen_ref.shape[1]
    f32 = jnp.float32
    note = jnp.concatenate([b[:, width:].astype(f32) for b in blocks], axis=0)
    plane = note.shape[0]
    ids = note[:, :fanout]
    gate = (
        note[:, fanout : 2 * fanout]
        + note[:, 2 * fanout : 3 * fanout]
        + note[:, 3 * fanout : 4 * fanout]
    )
    places = RING * capacity
    lane = lax.broadcasted_iota(jnp.int32, (plane, places), 1)
    row = lax.broadcasted_iota(jnp.int32, (plane, plane), 0)
    earlier = (lax.broadcasted_iota(jnp.int32, (plane, plane), 1) < row).astype(f32)
    taken = jnp.zeros((plane, places), f32)
    mixing = jnp.zeros((plane, places), f32)
    for j in range(RING):
        named = ids == column_ref[j].astype(f32)
        hit = jnp.max(jnp.where(named, 1.0, 0.0), axis=1, keepdims=True)
        weight = jnp.sum(jnp.where(named, gate, 0.0), axis=1, keepdims=True)
        rank = jnp.dot(
            earlier, jnp.broadcast_to(hit, (plane, NOTE)), preferred_element_type=f32
        )[:, :1]
        mark = (lane == rank.astype(jnp.int32) + j * capacity) & (lane >= j * capacity)
        mark = mark & (lane < (j + 1) * capacity) & (hit > 0.5)
        taken = jnp.where(mark, 1.0, taken)
        mixing = jnp.where(mark, weight, mixing)
    mixing_ref[...] = mixing
    taken = taken.astype(jnp.bfloat16)
    for low in range(0, width, chunk):
        held = jnp.concatenate([b[:, low : low + chunk] for b in blocks], axis=0)
        chosen_ref[:, low : low + chunk] = lax.dot_general(
            taken, held, (((0,), (0,)), ((), ())), preferred_element_type=f32
        ).astype(jnp.bfloat16)


def whole(kernel, out_shape, work, *operands, scalars=()):
    return pl.pallas_call(
        kernel,
        out_shape=out_shape,
        in_specs=[pl.BlockSpec(memory_space=pltpu.SMEM)] * len(scalars)
        + [pl.BlockSpec(memory_space=pltpu.VMEM)] * len(operands),
        out_specs=jax.tree.map(lambda _: pl.BlockSpec(memory_space=pltpu.VMEM), out_shape),
        compiler_params=pltpu.CompilerParams(vmem_limit_bytes=40 << 20),
        cost_estimate=pl.CostEstimate(flops=work, bytes_accessed=1 << 20, transcendentals=0),
    )(*scalars, *operands)


def stack_kernel(*refs):
    low = 0
    for ref in refs[:-1]:
        refs[-1][low : low + ref.shape[0]] = ref[...]
        low += ref.shape[0]


def gated_kernel(chunk, mixing_ref, *refs):
    blocks, (own_ref, *part_refs) = refs[:RING], refs[RING:]
    pieces, rest = [], mixing_ref[...]
    for _ in range(3):
        piece = rest.astype(jnp.bfloat16)
        pieces.append(piece)
        rest = rest - piece.astype(jnp.float32)
    line = own_ref.shape[0]
    for low in range(0, own_ref.shape[1], chunk):
        span = slice(low, low + chunk)
        back = jnp.concatenate([b[:, span] for b in blocks], axis=0)
        total = jnp.dot(pieces[0], back, preferred_element_type=jnp.float32)
        for piece in pieces[1:]:
            total = total + jnp.dot(piece, back, preferred_element_type=jnp.float32)
        own_ref[:, span] = total[:line]
        for n, part_ref in enumerate(part_refs):
            low_row = (n + 1) * line
            part_ref[:, span] = total[low_row : low_row + line].astype(jnp.bfloat16)


def sum_kernel(own_ref, *refs):
    total = own_ref[...]
    for ref in refs[: RING - 1]:
        total = total + ref[...].astype(jnp.float32)
    low = 0
    for ref in refs[RING - 1 :]:
        ref[...] = total[low : low + ref.shape[0]].astype(ref.dtype)
        low += ref.shape[0]


def expert_kernel(chunk, rows_ref, gate_ref, up_ref, down_ref, out_ref):
    f32 = jnp.float32
    gate_act = jnp.dot(rows_ref[...], gate_ref[0], preferred_element_type=f32)
    up_act = jnp.dot(rows_ref[...], up_ref[0], preferred_element_type=f32)
    hidden = (gate_act / (1.0 + jnp.exp(-gate_act)) * up_act).astype(jnp.bfloat16)
    for low in range(0, out_ref.shape[1], chunk):
        out_ref[:, low : low + chunk] = lax.dot_general(
            hidden,
            down_ref[0, low : low + chunk],
            (((1,), (1,)), ((), ())),
            preferred_element_type=f32,
        ).astype(out_ref.dtype)


def add_kernel(one_ref, two_ref, out_ref):
    out_ref[...] = (one_ref[...] + two_ref[...].astype(jnp.float32)).astype(out_ref.dtype)


def copy_kernel(from_ref, to_ref, held, came, went):
    share = held.shape[1]
    spans = [pl.ds(n * share, share) for n in range(held.shape[0])]
    inward = [
        pltpu.make_async_copy(from_ref.at[0, span], held.at[n], came.at[n])
        for n, span in enumerate(spans)
    ]
    outward = [
        pltpu.make_async_copy(held.at[n], to_ref.at[0, span], went.at[n])
        for n, span in enumerate(spans)
    ]
    for copy in inward:
        copy.start()
    for first, second in zip(inward, outward):
        first.wait()
        second.start()
    for copy in outward:
        copy.wait()


def copied(value):
    parts, (_, depth, units) = 8, value.shape
    return pl.pallas_call(
        copy_kernel,
        out_shape=jax.ShapeDtypeStruct(value.shape, value.dtype),
        in_specs=[pl.BlockSpec(memory_space=pl.ANY)],
        out_specs=pl.BlockSpec(memory_space=pl.ANY),
        scratch_shapes=[
            pltpu.VMEM((parts, depth // parts, units), value.dtype),
            pltpu.SemaphoreType.DMA((parts,)),
            pltpu.SemaphoreType.DMA((parts,)),
        ],
        compiler_params=pltpu.CompilerParams(vmem_limit_bytes=16 << 20),
        cost_estimate=pl.CostEstimate(flops=0, bytes_accessed=8 << 20, transcendentals=0),
    )(value)


def on_device(tokens, gates, top_ids, home_expert, copy_source, home_gate, home_up, home_down):
    experts = lax.axis_size("expert")
    rows, width = tokens.shape
    fanout = top_ids.shape[1]
    most = (rows * fanout + experts - 1) // experts + 1
    capacity = 4 * RING * most
    depth, units = home_gate.shape[1:]
    blocked = (experts, depth // experts, units)
    here = lax.axis_index("expert")
    core = lax.axis_index("attn") % 2
    z, y, x_hi = here // (2 * RING), here // 2 % RING, here % 2
    bf16, f32 = jnp.bfloat16, jnp.float32
    ahead = jnp.arange(RING, dtype=jnp.int32)
    column = ((z + ahead * (1 - core)) % RING * RING + (y + ahead * core) % RING) * 2 + x_hi
    column_expert = home_expert[column]
    tie = lax.optimization_barrier

    note = jnp.concatenate([top_ids.astype(bf16)] + bf16_pieces(gates), axis=1)
    note = jnp.pad(note, ((0, 0), (0, NOTE - note.shape[1])))
    held, gate_blocks = tie((jnp.concatenate([tokens, note], axis=1), home_gate.reshape(blocked)))
    near = [send(held, row_step(n)) for n in range(1, 4)]
    gate_spread = swap_blocks(gate_blocks)
    line = 4 * rows
    held = whole(
        stack_kernel, jax.ShapeDtypeStruct((line, width + NOTE), bf16), WORK, held, *near
    )

    held, up_blocks, gate_spread = tie((held, home_up.reshape(blocked), gate_spread))
    blocks = [held] + [send(held, wide_step(n)) for n in range(1, RING)]
    up_spread = swap_blocks(up_blocks)
    blocks, gate_spread = tie((blocks, gate_spread))
    blocks, gate_picks = tie((blocks, gate_spread[copy_source]))
    places = RING * capacity
    chosen, mixing = whole(
        functools.partial(select_kernel, fanout, capacity, width // 8),
        (
            jax.ShapeDtypeStruct((places, width), bf16),
            jax.ShapeDtypeStruct((RING * line, places), f32),
        ),
        WORK,
        *blocks,
        scalars=(column_expert,),
    )

    chosen, down_blocks, up_spread = tie((chosen, home_down.reshape(blocked), up_spread))
    chosen = chosen.reshape(RING, capacity, width)
    mine = [chosen[0]] + [send(chosen[n], deep_step(n)) for n in range(1, RING)]
    down_spread = swap_blocks(down_blocks)
    mine = whole(stack_kernel, jax.ShapeDtypeStruct((places, width), bf16), WORK, *mine)

    mine, gate_picks, down_spread = tie((mine, gate_picks, down_spread))
    other = send(mine, CORE_SWAP)
    replica_gate = swap_blocks(gate_picks)
    other, up_spread, down_spread = tie((other, up_spread, down_spread))
    other, up_picks, down_picks = tie((other, up_spread[copy_source], down_spread[copy_source]))

    def expert_part(slot_rows, dtype):
        return whole(
            functools.partial(expert_kernel, width // 8),
            jax.ShapeDtypeStruct((places, width), dtype),
            WORK,
            slot_rows,
            home_gate,
            home_up,
            home_down,
        )

    given = send(expert_part(other, bf16), CORE_SWAP)
    summed = whole(
        add_kernel,
        jax.ShapeDtypeStruct((places, width), bf16),
        1 << 20,
        expert_part(mine, f32),
        given,
    )

    summed, up_picks, replica_gate = tie((summed, up_picks, replica_gate))
    summed = summed.reshape(RING, capacity, width)
    back = [summed[0]] + [send(summed[n], deep_step(-n)) for n in range(1, RING)]
    replica_up = swap_blocks(up_picks)
    own, *parts = whole(
        functools.partial(gated_kernel, width // 8),
        (jax.ShapeDtypeStruct((line, width), f32),)
        + (jax.ShapeDtypeStruct((line, width), bf16),) * (RING - 1),
        WORK,
        mixing,
        *back,
    )

    parts, down_picks, replica_up = tie((parts, down_picks, replica_up))
    parts = [send(parts[n - 1], wide_step(-n)) for n in range(1, RING)]
    replica_down = swap_blocks(down_picks)
    replica_gate = copied(replica_gate.reshape(1, depth, units))
    replica_up = copied(replica_up.reshape(1, depth, units))
    parts, replica_gate, replica_up = tie((parts, replica_gate, replica_up))
    own, *parts = whole(
        sum_kernel,
        (jax.ShapeDtypeStruct((rows, width), f32),)
        + (jax.ShapeDtypeStruct((rows, width), bf16),) * 3,
        WORK,
        own,
        *parts,
    )

    parts, replica_down = tie((parts, replica_down))
    parts = [send(parts[n - 1], row_step(n)) for n in range(1, 4)]
    replica_down = copied(replica_down.reshape(1, depth, units))
    mixed = whole(sum_kernel, (jax.ShapeDtypeStruct((rows, width), bf16),), 1 << 20, own, *parts)[0]
    return (mixed, replica_gate, replica_up, replica_down)


def solution(mesh):
    row_spec = P(("attn", "expert"), None)
    weight_spec = P("expert", None, "attn")
    return jax.shard_map(
        on_device,
        mesh=mesh,
        in_specs=(row_spec, row_spec, row_spec, P(), P(), weight_spec, weight_spec, weight_spec),
        out_specs=(row_spec, weight_spec, weight_spec, weight_spec),
        check_vma=False,
    )
```

```python
import functools

import jax
import jax.numpy as jnp
from jax import lax
from jax.experimental import pallas as pl
from jax.experimental.pallas import tpu as pltpu
from jax.sharding import PartitionSpec as P

RING = 4
NOTE = 128
EXPERT_AXIS = RING * RING * 2
WORK = 1 << 36
BOTH = ("attn", "expert")


def table(step):
    pairs = []
    for x_lo in range(2):
        for core in range(2):
            for z in range(RING):
                for y in range(RING):
                    for x_hi in range(2):
                        to = step(x_lo, core, z, y, x_hi)
                        ends = []
                        for a, c, k, j, i in ((x_lo, core, z, y, x_hi), to):
                            slot = ((k % RING) * RING + j % RING) * 2 + i % 2
                            ends.append(((a % 2) * 2 + c % 2) * EXPERT_AXIS + slot)
                        pairs.append(tuple(ends))
    return pairs


def row_step(n):
    return table(lambda a, c, z, y, x: (a + n % 2, c, z, y, x + n // 2))


def wide_step(n):
    return table(lambda a, c, z, y, x: (a, c, z + n * c, y + n * (1 - c), x))


def deep_step(n):
    return table(lambda a, c, z, y, x: (a, c, z + n * (1 - c), y + n * c, x))


CORE_SWAP = table(lambda a, c, z, y, x: (a, c + 1, z, y, x))


def send(value, pairs):
    return lax.ppermute(value, BOTH, pairs)


def swap_blocks(blocks):
    return lax.all_to_all(blocks, "expert", split_axis=0, concat_axis=0, tiled=True)


def bf16_pieces(values):
    pieces, rest = [], values
    for _ in range(3):
        piece = lax.reduce_precision(rest, exponent_bits=8, mantissa_bits=7)
        pieces.append(piece.astype(jnp.bfloat16))
        rest = rest - piece
    return pieces


def select_kernel(fanout, capacity, chunk, column_ref, *refs):
    blocks, (chosen_ref, mixing_ref) = refs[:RING], refs[RING:]
    width = chosen_ref.shape[1]
    f32 = jnp.float32
    note = jnp.concatenate([b[:, width:].astype(f32) for b in blocks], axis=0)
    plane = note.shape[0]
    ids = note[:, :fanout]
    gate = (
        note[:, fanout : 2 * fanout]
        + note[:, 2 * fanout : 3 * fanout]
        + note[:, 3 * fanout : 4 * fanout]
    )
    places = RING * capacity
    lane = lax.broadcasted_iota(jnp.int32, (plane, places), 1)
    row = lax.broadcasted_iota(jnp.int32, (plane, plane), 0)
    earlier = (lax.broadcasted_iota(jnp.int32, (plane, plane), 1) < row).astype(f32)
    taken = jnp.zeros((plane, places), f32)
    mixing = jnp.zeros((plane, places), f32)
    for j in range(RING):
        named = ids == column_ref[j].astype(f32)
        hit = jnp.max(jnp.where(named, 1.0, 0.0), axis=1, keepdims=True)
        weight = jnp.sum(jnp.where(named, gate, 0.0), axis=1, keepdims=True)
        rank = jnp.dot(
            earlier, jnp.broadcast_to(hit, (plane, NOTE)), preferred_element_type=f32
        )[:, :1]
        mark = (lane == rank.astype(jnp.int32) + j * capacity) & (lane >= j * capacity)
        mark = mark & (lane < (j + 1) * capacity) & (hit > 0.5)
        taken = jnp.where(mark, 1.0, taken)
        mixing = jnp.where(mark, weight, mixing)
    mixing_ref[...] = mixing
    taken = taken.astype(jnp.bfloat16)
    for low in range(0, width, chunk):
        held = jnp.concatenate([b[:, low : low + chunk] for b in blocks], axis=0)
        chosen_ref[:, low : low + chunk] = lax.dot_general(
            taken, held, (((0,), (0,)), ((), ())), preferred_element_type=f32
        ).astype(jnp.bfloat16)


def whole(kernel, out_shape, work, *operands, scalars=()):
    return pl.pallas_call(
        kernel,
        out_shape=out_shape,
        in_specs=[pl.BlockSpec(memory_space=pltpu.SMEM)] * len(scalars)
        + [pl.BlockSpec(memory_space=pltpu.VMEM)] * len(operands),
        out_specs=jax.tree.map(lambda _: pl.BlockSpec(memory_space=pltpu.VMEM), out_shape),
        compiler_params=pltpu.CompilerParams(vmem_limit_bytes=40 << 20),
        cost_estimate=pl.CostEstimate(flops=work, bytes_accessed=1 << 20, transcendentals=0),
    )(*scalars, *operands)


def stack_kernel(*refs):
    low = 0
    for ref in refs[:-1]:
        refs[-1][low : low + ref.shape[0]] = ref[...]
        low += ref.shape[0]


def gated_kernel(chunk, mixing_ref, *refs):
    blocks, (own_ref, *part_refs) = refs[:RING], refs[RING:]
    pieces, rest = [], mixing_ref[...]
    for _ in range(3):
        piece = rest.astype(jnp.bfloat16)
        pieces.append(piece)
        rest = rest - piece.astype(jnp.float32)
    line = own_ref.shape[0]
    for low in range(0, own_ref.shape[1], chunk):
        span = slice(low, low + chunk)
        back = jnp.concatenate([b[:, span] for b in blocks], axis=0)
        total = jnp.dot(pieces[0], back, preferred_element_type=jnp.float32)
        for piece in pieces[1:]:
            total = total + jnp.dot(piece, back, preferred_element_type=jnp.float32)
        own_ref[:, span] = total[:line]
        for n, part_ref in enumerate(part_refs):
            low_row = (n + 1) * line
            part_ref[:, span] = total[low_row : low_row + line].astype(jnp.bfloat16)


def sum_kernel(own_ref, *refs):
    total = own_ref[...]
    for ref in refs[: RING - 1]:
        total = total + ref[...].astype(jnp.float32)
    low = 0
    for ref in refs[RING - 1 :]:
        ref[...] = total[low : low + ref.shape[0]].astype(ref.dtype)
        low += ref.shape[0]


def expert_kernel(chunk, rows_ref, gate_ref, up_ref, down_ref, out_ref):
    f32 = jnp.float32
    gate_act = jnp.dot(rows_ref[...], gate_ref[0], preferred_element_type=f32)
    up_act = jnp.dot(rows_ref[...], up_ref[0], preferred_element_type=f32)
    hidden = (gate_act / (1.0 + jnp.exp(-gate_act)) * up_act).astype(jnp.bfloat16)
    for low in range(0, out_ref.shape[1], chunk):
        out_ref[:, low : low + chunk] = lax.dot_general(
            hidden,
            down_ref[0, low : low + chunk],
            (((1,), (1,)), ((), ())),
            preferred_element_type=f32,
        ).astype(out_ref.dtype)


def add_kernel(one_ref, two_ref, out_ref):
    out_ref[...] = (one_ref[...] + two_ref[...].astype(jnp.float32)).astype(out_ref.dtype)


def pick_kernel(source_ref, *refs):
    refs[-1][...] = refs[0][...]


def picked(copy_source, spread):
    count, height, units = spread.shape
    return pl.pallas_call(
        pick_kernel,
        out_shape=jax.ShapeDtypeStruct(spread.shape, spread.dtype),
        grid_spec=pltpu.PrefetchScalarGridSpec(
            num_scalar_prefetch=1,
            grid=(count,),
            in_specs=[pl.BlockSpec((1, height, units), lambda i, s: (s[i], 0, 0))],
            out_specs=pl.BlockSpec((1, height, units), lambda i, s: (i, 0, 0)),
        ),
        cost_estimate=pl.CostEstimate(flops=0, bytes_accessed=1 << 20, transcendentals=0),
    )(copy_source, spread)


def swap_cores(value, parts=4):
    rows = value.shape[0] // parts
    return jnp.concatenate(
        [send(value[n * rows : (n + 1) * rows], CORE_SWAP) for n in range(parts)], axis=0
    )


def copy_kernel(from_ref, to_ref, held, came, went):
    share = held.shape[1]
    spans = [pl.ds(n * share, share) for n in range(held.shape[0])]
    inward = [
        pltpu.make_async_copy(from_ref.at[0, span], held.at[n], came.at[n])
        for n, span in enumerate(spans)
    ]
    outward = [
        pltpu.make_async_copy(held.at[n], to_ref.at[0, span], went.at[n])
        for n, span in enumerate(spans)
    ]
    for copy in inward:
        copy.start()
    for first, second in zip(inward, outward):
        first.wait()
        second.start()
    for copy in outward:
        copy.wait()


def copied(value):
    parts, (_, depth, units) = 8, value.shape
    return pl.pallas_call(
        copy_kernel,
        out_shape=jax.ShapeDtypeStruct(value.shape, value.dtype),
        in_specs=[pl.BlockSpec(memory_space=pl.ANY)],
        out_specs=pl.BlockSpec(memory_space=pl.ANY),
        scratch_shapes=[
            pltpu.VMEM((parts, depth // parts, units), value.dtype),
            pltpu.SemaphoreType.DMA((parts,)),
            pltpu.SemaphoreType.DMA((parts,)),
        ],
        compiler_params=pltpu.CompilerParams(vmem_limit_bytes=16 << 20),
        cost_estimate=pl.CostEstimate(flops=0, bytes_accessed=8 << 20, transcendentals=0),
    )(value)


def on_device(tokens, gates, top_ids, home_expert, copy_source, home_gate, home_up, home_down):
    experts = lax.axis_size("expert")
    rows, width = tokens.shape
    fanout = top_ids.shape[1]
    most = (rows * fanout + experts - 1) // experts + 1
    capacity = 4 * RING * most
    depth, units = home_gate.shape[1:]
    blocked = (experts, depth // experts, units)
    here = lax.axis_index("expert")
    core = lax.axis_index("attn") % 2
    z, y, x_hi = here // (2 * RING), here // 2 % RING, here % 2
    bf16, f32 = jnp.bfloat16, jnp.float32
    ahead = jnp.arange(RING, dtype=jnp.int32)
    column = ((z + ahead * (1 - core)) % RING * RING + (y + ahead * core) % RING) * 2 + x_hi
    column_expert = home_expert[column]
    tie = lax.optimization_barrier

    note = jnp.concatenate([top_ids.astype(bf16)] + bf16_pieces(gates), axis=1)
    note = jnp.pad(note, ((0, 0), (0, NOTE - note.shape[1])))
    held, gate_blocks = tie((jnp.concatenate([tokens, note], axis=1), home_gate.reshape(blocked)))
    near = [send(held, row_step(n)) for n in range(1, 4)]
    gate_spread = swap_blocks(gate_blocks)
    line = 4 * rows
    held = whole(
        stack_kernel, jax.ShapeDtypeStruct((line, width + NOTE), bf16), WORK, held, *near
    )

    blocks = [held] + [send(held, wide_step(n)) for n in range(1, RING)]
    both = jnp.concatenate([home_up.reshape(blocked), home_down.reshape(blocked)], axis=1)
    both, gate_spread = tie((both, gate_spread))
    both_spread = swap_blocks(both)
    gate_picks = gate_spread[copy_source]
    places = RING * capacity
    chosen, mixing = whole(
        functools.partial(select_kernel, fanout, capacity, width // 8),
        (
            jax.ShapeDtypeStruct((places, width), bf16),
            jax.ShapeDtypeStruct((RING * line, places), f32),
        ),
        WORK >> 3,
        *blocks,
        scalars=(column_expert,),
    )

    chosen = chosen.reshape(RING, capacity, width)
    mine = [chosen[0]] + [send(chosen[n], deep_step(n)) for n in range(1, RING)]
    gate_picks, both_spread = tie((gate_picks, both_spread))
    replica_gate = swap_blocks(gate_picks)
    both_picks = picked(copy_source, both_spread)
    mine = whole(stack_kernel, jax.ShapeDtypeStruct((places, width), bf16), WORK, *mine)
    other = swap_cores(mine)

    def expert_part(slot_rows, dtype):
        return whole(
            functools.partial(expert_kernel, width // 8),
            jax.ShapeDtypeStruct((places, width), dtype),
            1 << 20,
            slot_rows,
            home_gate,
            home_up,
            home_down,
        )

    given = swap_cores(expert_part(other, bf16))
    summed = whole(
        add_kernel,
        jax.ShapeDtypeStruct((places, width), bf16),
        1 << 20,
        expert_part(mine, f32),
        given,
    )

    summed = summed.reshape(RING, capacity, width)
    back = [summed[0]] + [send(summed[n], deep_step(-n)) for n in range(1, RING)]
    both_picks, replica_gate = tie((both_picks, replica_gate))
    replica_both = swap_blocks(both_picks)
    replica_gate = copied(replica_gate.reshape(1, depth, units))
    mixing, replica_gate = tie((mixing, replica_gate))
    own, *parts = whole(
        functools.partial(gated_kernel, width // 8),
        (jax.ShapeDtypeStruct((line, width), f32),)
        + (jax.ShapeDtypeStruct((line, width), bf16),) * (RING - 1),
        WORK,
        mixing,
        *back,
    )
    parts = [send(parts[n - 1], wide_step(-n)) for n in range(1, RING)]
    own, *parts = whole(
        sum_kernel,
        (jax.ShapeDtypeStruct((rows, width), f32),)
        + (jax.ShapeDtypeStruct((rows, width), bf16),) * 3,
        1 << 20,
        own,
        *parts,
    )

    parts, replica_both = tie((parts, replica_both))
    parts = [send(parts[n - 1], row_step(n)) for n in range(1, 4)]
    share = depth // experts
    replica_up = replica_both[:, :share].reshape(1, depth, units)
    replica_down = replica_both[:, share:].reshape(1, depth, units)
    mixed = whole(sum_kernel, (jax.ShapeDtypeStruct((rows, width), bf16),), 1 << 20, own, *parts)[0]
    return (mixed, replica_gate, replica_up, replica_down)


def solution(mesh):
    row_spec = P(("attn", "expert"), None)
    weight_spec = P("expert", None, "attn")
    return jax.shard_map(
        on_device,
        mesh=mesh,
        in_specs=(row_spec, row_spec, row_spec, P(), P(), weight_spec, weight_spec, weight_spec),
        out_specs=(row_spec, weight_spec, weight_spec, weight_spec),
        check_vma=False,
    )
```

```python
import functools

import jax
import jax.numpy as jnp
from jax import lax
from jax.experimental import pallas as pl
from jax.experimental.pallas import tpu as pltpu
from jax.sharding import PartitionSpec as P

RING = 4
NOTE = 128
EXPERT_AXIS = RING * RING * 2
WORK = 1 << 36
BOTH = ("attn", "expert")


def table(step):
    pairs = []
    for x_lo in range(2):
        for core in range(2):
            for z in range(RING):
                for y in range(RING):
                    for x_hi in range(2):
                        to = step(x_lo, core, z, y, x_hi)
                        ends = []
                        for a, c, k, j, i in ((x_lo, core, z, y, x_hi), to):
                            slot = ((k % RING) * RING + j % RING) * 2 + i % 2
                            ends.append(((a % 2) * 2 + c % 2) * EXPERT_AXIS + slot)
                        pairs.append(tuple(ends))
    return pairs


def row_step(n):
    return table(lambda a, c, z, y, x: (a + n % 2, c, z, y, x + n // 2))


def wide_step(n):
    return table(lambda a, c, z, y, x: (a, c, z + n * c, y + n * (1 - c), x))


def deep_step(n):
    return table(lambda a, c, z, y, x: (a, c, z + n * (1 - c), y + n * c, x))


CORE_SWAP = table(lambda a, c, z, y, x: (a, c + 1, z, y, x))


def send(value, pairs):
    return lax.ppermute(value, BOTH, pairs)


def swap_blocks(blocks):
    return lax.all_to_all(blocks, "expert", split_axis=0, concat_axis=0, tiled=True)


def bf16_pieces(values):
    pieces, rest = [], values
    for _ in range(3):
        piece = lax.reduce_precision(rest, exponent_bits=8, mantissa_bits=7)
        pieces.append(piece.astype(jnp.bfloat16))
        rest = rest - piece
    return pieces


def select_kernel(fanout, capacity, chunk, column_ref, *refs):
    blocks, (*chosen_refs, mixing_ref) = refs[:RING], refs[RING:]
    width = chosen_refs[0].shape[1]
    f32 = jnp.float32
    note = jnp.concatenate([b[:, width:].astype(f32) for b in blocks], axis=0)
    plane = note.shape[0]
    ids = note[:, :fanout]
    gate = (
        note[:, fanout : 2 * fanout]
        + note[:, 2 * fanout : 3 * fanout]
        + note[:, 3 * fanout : 4 * fanout]
    )
    places = RING * capacity
    lane = lax.broadcasted_iota(jnp.int32, (plane, places), 1)
    row = lax.broadcasted_iota(jnp.int32, (plane, plane), 0)
    earlier = (lax.broadcasted_iota(jnp.int32, (plane, plane), 1) < row).astype(f32)
    taken = jnp.zeros((plane, places), f32)
    mixing = jnp.zeros((plane, places), f32)
    for j in range(RING):
        named = ids == column_ref[j].astype(f32)
        hit = jnp.max(jnp.where(named, 1.0, 0.0), axis=1, keepdims=True)
        weight = jnp.sum(jnp.where(named, gate, 0.0), axis=1, keepdims=True)
        rank = jnp.dot(
            earlier, jnp.broadcast_to(hit, (plane, NOTE)), preferred_element_type=f32
        )[:, :1]
        mark = (lane == rank.astype(jnp.int32) + j * capacity) & (lane >= j * capacity)
        mark = mark & (lane < (j + 1) * capacity) & (hit > 0.5)
        taken = jnp.where(mark, 1.0, taken)
        mixing = jnp.where(mark, weight, mixing)
    mixing_ref[...] = mixing
    taken = taken.astype(jnp.bfloat16)
    for low in range(0, width, chunk):
        held = jnp.concatenate([b[:, low : low + chunk] for b in blocks], axis=0)
        chosen = lax.dot_general(
            taken, held, (((0,), (0,)), ((), ())), preferred_element_type=f32
        ).astype(jnp.bfloat16)
        for n, chosen_ref in enumerate(chosen_refs):
            chosen_ref[:, low : low + chunk] = chosen[n * capacity : (n + 1) * capacity]


def whole(kernel, out_shape, work, *operands, scalars=()):
    return pl.pallas_call(
        kernel,
        out_shape=out_shape,
        in_specs=[pl.BlockSpec(memory_space=pltpu.SMEM)] * len(scalars)
        + [pl.BlockSpec(memory_space=pltpu.VMEM)] * len(operands),
        out_specs=jax.tree.map(lambda _: pl.BlockSpec(memory_space=pltpu.VMEM), out_shape),
        compiler_params=pltpu.CompilerParams(vmem_limit_bytes=48 << 20),
        cost_estimate=pl.CostEstimate(flops=work, bytes_accessed=1 << 20, transcendentals=0),
    )(*scalars, *operands)


def stack_kernel(*refs):
    low = 0
    for ref in refs[:-1]:
        refs[-1][low : low + ref.shape[0]] = ref[...]
        low += ref.shape[0]


def gated_kernel(chunk, mixing_ref, *refs):
    blocks, (own_ref, *part_refs) = refs[:RING], refs[RING:]
    pieces, rest = [], mixing_ref[...]
    for _ in range(3):
        piece = rest.astype(jnp.bfloat16)
        pieces.append(piece)
        rest = rest - piece.astype(jnp.float32)
    line = own_ref.shape[0]
    for low in range(0, own_ref.shape[1], chunk):
        span = slice(low, low + chunk)
        back = jnp.concatenate([b[:, span] for b in blocks], axis=0)
        total = jnp.dot(pieces[0], back, preferred_element_type=jnp.float32)
        for piece in pieces[1:]:
            total = total + jnp.dot(piece, back, preferred_element_type=jnp.float32)
        own_ref[:, span] = total[:line]
        for n, part_ref in enumerate(part_refs):
            low_row = (n + 1) * line
            part_ref[:, span] = total[low_row : low_row + line].astype(jnp.bfloat16)


def sum_kernel(own_ref, *refs):
    total = own_ref[...]
    for ref in refs[: RING - 1]:
        total = total + ref[...].astype(jnp.float32)
    low = 0
    for ref in refs[RING - 1 :]:
        ref[...] = total[low : low + ref.shape[0]].astype(ref.dtype)
        low += ref.shape[0]


def expert_kernel(chunk, *refs):
    f32 = jnp.float32
    blocks, weights, outs = refs[:RING], refs[RING : RING + 6], refs[RING + 6 :]
    rows = jnp.concatenate([b[...] for b in blocks], axis=0)
    hidden = []
    for gate_ref, up_ref in (weights[:2], weights[3:5]):
        gate_act = jnp.dot(rows, gate_ref[0], preferred_element_type=f32)
        up_act = jnp.dot(rows, up_ref[0], preferred_element_type=f32)
        hidden.append((gate_act / (1.0 + jnp.exp(-gate_act)) * up_act).astype(jnp.bfloat16))
    height = outs[0].shape[0]
    for low in range(0, outs[0].shape[1], chunk):
        span = slice(low, low + chunk)
        total = 0.0
        for part, down_ref in zip(hidden, (weights[2], weights[5])):
            total = total + lax.dot_general(
                part, down_ref[0, span], (((1,), (1,)), ((), ())), preferred_element_type=f32
            )
        for n, out_ref in enumerate(outs):
            out_ref[:, span] = total[n * height : (n + 1) * height].astype(out_ref.dtype)


def pick_kernel(source_ref, from_ref, to_ref, held, came, went):
    count = held.shape[0]
    inward = [
        pltpu.make_async_copy(from_ref.at[source_ref[n]], held.at[n], came.at[n])
        for n in range(count)
    ]
    outward = [pltpu.make_async_copy(held.at[n], to_ref.at[n], went.at[n]) for n in range(count)]
    for copy in inward:
        copy.start()
    for first, second in zip(inward, outward):
        first.wait()
        second.start()
    for copy in outward:
        copy.wait()


def picked(copy_source, spread):
    count = spread.shape[0]
    return pl.pallas_call(
        pick_kernel,
        out_shape=jax.ShapeDtypeStruct(spread.shape, spread.dtype),
        in_specs=[pl.BlockSpec(memory_space=pltpu.SMEM), pl.BlockSpec(memory_space=pl.ANY)],
        out_specs=pl.BlockSpec(memory_space=pl.ANY),
        scratch_shapes=[
            pltpu.VMEM(spread.shape, spread.dtype),
            pltpu.SemaphoreType.DMA((count,)),
            pltpu.SemaphoreType.DMA((count,)),
        ],
        compiler_params=pltpu.CompilerParams(vmem_limit_bytes=16 << 20),
        cost_estimate=pl.CostEstimate(flops=0, bytes_accessed=1 << 20, transcendentals=0),
    )(copy_source, spread)


def copy_kernel(from_ref, to_ref, held, came, went):
    share = held.shape[1]
    spans = [pl.ds(n * share, share) for n in range(held.shape[0])]
    inward = [
        pltpu.make_async_copy(from_ref.at[0, span], held.at[n], came.at[n])
        for n, span in enumerate(spans)
    ]
    outward = [
        pltpu.make_async_copy(held.at[n], to_ref.at[0, span], went.at[n])
        for n, span in enumerate(spans)
    ]
    for copy in inward:
        copy.start()
    for first, second in zip(inward, outward):
        first.wait()
        second.start()
    for copy in outward:
        copy.wait()


def copied(value):
    parts, (_, depth, units) = 8, value.shape
    return pl.pallas_call(
        copy_kernel,
        out_shape=jax.ShapeDtypeStruct(value.shape, value.dtype),
        in_specs=[pl.BlockSpec(memory_space=pl.ANY)],
        out_specs=pl.BlockSpec(memory_space=pl.ANY),
        scratch_shapes=[
            pltpu.VMEM((parts, depth // parts, units), value.dtype),
            pltpu.SemaphoreType.DMA((parts,)),
            pltpu.SemaphoreType.DMA((parts,)),
        ],
        compiler_params=pltpu.CompilerParams(vmem_limit_bytes=16 << 20),
        cost_estimate=pl.CostEstimate(flops=0, bytes_accessed=8 << 20, transcendentals=0),
    )(value)


def on_device(tokens, gates, top_ids, home_expert, copy_source, home_gate, home_up, home_down):
    experts = lax.axis_size("expert")
    rows, width = tokens.shape
    fanout = top_ids.shape[1]
    most = (rows * fanout + experts - 1) // experts + 1
    capacity = 4 * RING * most
    depth, units = home_gate.shape[1:]
    blocked = (experts, depth // experts, units)
    here = lax.axis_index("expert")
    core = lax.axis_index("attn") % 2
    z, y, x_hi = here // (2 * RING), here // 2 % RING, here % 2
    bf16, f32 = jnp.bfloat16, jnp.float32
    ahead = jnp.arange(RING, dtype=jnp.int32)
    column = ((z + ahead * (1 - core)) % RING * RING + (y + ahead * core) % RING) * 2 + x_hi
    column_expert = home_expert[column]
    tie = lax.optimization_barrier

    note = jnp.concatenate([top_ids.astype(bf16)] + bf16_pieces(gates), axis=1)
    note = jnp.pad(note, ((0, 0), (0, NOTE - note.shape[1])))
    held, gate_blocks = tie((jnp.concatenate([tokens, note], axis=1), home_gate.reshape(blocked)))
    near = [send(held, row_step(n)) for n in range(1, RING)]
    gate_spread = swap_blocks(gate_blocks)
    both = jnp.concatenate([home_up.reshape(blocked), home_down.reshape(blocked)], axis=1)
    near, far_gate = tie((near, send(home_gate, CORE_SWAP)))
    line = RING * rows
    held = whole(
        stack_kernel, jax.ShapeDtypeStruct((line, width + NOTE), bf16), WORK, held, *near
    )

    blocks = [held] + [send(held, wide_step(n)) for n in range(1, RING)]
    far = (send(home_up, CORE_SWAP), send(home_down, CORE_SWAP))
    blocks, far = tie((blocks, far))
    places = RING * capacity
    *chosen, mixing = whole(
        functools.partial(select_kernel, fanout, capacity, width // 8),
        (jax.ShapeDtypeStruct((capacity, width), bf16),) * RING
        + (jax.ShapeDtypeStruct((RING * line, places), f32),),
        WORK,
        *blocks,
        scalars=(column_expert,),
    )

    both, gate_spread, mixing = tie((both, gate_spread, mixing))
    both_spread = swap_blocks(both)

    mine = [chosen[0]] + [send(chosen[n], deep_step(n)) for n in range(1, RING)]
    summed = whole(
        functools.partial(expert_kernel, width // 8),
        (jax.ShapeDtypeStruct((capacity, width), bf16),) * RING,
        WORK,
        *mine,
        home_gate,
        home_up,
        home_down,
        far_gate,
        *far,
    )
    gate_picks = gate_spread[copy_source]
    gate_picks, both_spread, _ = tie((gate_picks, both_spread, summed[0]))
    replica_gate = swap_blocks(gate_picks)

    back = [summed[0]] + [send(summed[n], deep_step(-n)) for n in range(1, RING)]
    own, *parts = whole(
        functools.partial(gated_kernel, width // 8),
        (jax.ShapeDtypeStruct((line, width), f32),)
        + (jax.ShapeDtypeStruct((line, width), bf16),) * (RING - 1),
        WORK,
        mixing,
        *back,
    )
    parts = [send(parts[n - 1], wide_step(-n)) for n in range(1, RING)]
    both_spread, own = tie((both_spread, own))
    own, both_picks = tie((own, picked(copy_source, both_spread)))
    own, *parts = whole(
        sum_kernel,
        (jax.ShapeDtypeStruct((rows, width), f32),)
        + (jax.ShapeDtypeStruct((rows, width), bf16),) * 3,
        1 << 20,
        own,
        *parts,
    )

    both_picks, replica_gate, own = tie((both_picks, replica_gate, own))
    replica_both = swap_blocks(both_picks)
    replica_gate = copied(replica_gate.reshape(1, depth, units))
    own, replica_gate = tie((own, replica_gate))
    parts = [send(parts[n - 1], row_step(n)) for n in range(1, RING)]
    share = depth // experts
    replica_up = replica_both[:, :share].reshape(1, depth, units)
    replica_down = replica_both[:, share:].reshape(1, depth, units)
    mixed = whole(sum_kernel, (jax.ShapeDtypeStruct((rows, width), bf16),), 1 << 20, own, *parts)[0]
    return (mixed, replica_gate, replica_up, replica_down)


def solution(mesh):
    row_spec = P(("attn", "expert"), None)
    weight_spec = P("expert", None, "attn")
    return jax.shard_map(
        on_device,
        mesh=mesh,
        in_specs=(row_spec, row_spec, row_spec, P(), P(), weight_spec, weight_spec, weight_spec),
        out_specs=(row_spec, weight_spec, weight_spec, weight_spec),
        check_vma=False,
    )
```

```python
import functools

import jax
import jax.numpy as jnp
from jax import lax
from jax.experimental import pallas as pl
from jax.experimental.pallas import tpu as pltpu
from jax.sharding import PartitionSpec as P

RING = 4
NOTE = 128
EXPERT_AXIS = RING * RING * 2
WORK = 1 << 36
BOTH = ("attn", "expert")


def table(step):
    pairs = []
    for x_lo in range(2):
        for core in range(2):
            for z in range(RING):
                for y in range(RING):
                    for x_hi in range(2):
                        to = step(x_lo, core, z, y, x_hi)
                        ends = []
                        for a, c, k, j, i in ((x_lo, core, z, y, x_hi), to):
                            slot = ((k % RING) * RING + j % RING) * 2 + i % 2
                            ends.append(((a % 2) * 2 + c % 2) * EXPERT_AXIS + slot)
                        pairs.append(tuple(ends))
    return pairs


def row_step(n):
    return table(lambda a, c, z, y, x: (a + n % 2, c, z, y, x + n // 2))


def wide_step(n):
    return table(lambda a, c, z, y, x: (a, c, z + n * c, y + n * (1 - c), x))


def deep_step(n):
    return table(lambda a, c, z, y, x: (a, c, z + n * (1 - c), y + n * c, x))


CORE_SWAP = table(lambda a, c, z, y, x: (a, c + 1, z, y, x))


def send(value, pairs):
    return lax.ppermute(value, BOTH, pairs)


def swap_blocks(blocks):
    return lax.all_to_all(blocks, "expert", split_axis=0, concat_axis=0, tiled=True)


def bf16_pieces(values):
    pieces, rest = [], values
    for _ in range(3):
        piece = lax.reduce_precision(rest, exponent_bits=8, mantissa_bits=7)
        pieces.append(piece.astype(jnp.bfloat16))
        rest = rest - piece
    return pieces


def select_kernel(fanout, capacity, chunk, column_ref, *refs):
    blocks, (*chosen_refs, mixing_ref) = refs[:RING], refs[RING:]
    width = chosen_refs[0].shape[1]
    f32 = jnp.float32
    note = jnp.concatenate([b[:, width:].astype(f32) for b in blocks], axis=0)
    plane = note.shape[0]
    ids = note[:, :fanout]
    gate = (
        note[:, fanout : 2 * fanout]
        + note[:, 2 * fanout : 3 * fanout]
        + note[:, 3 * fanout : 4 * fanout]
    )
    places = RING * capacity
    lane = lax.broadcasted_iota(jnp.int32, (plane, places), 1)
    row = lax.broadcasted_iota(jnp.int32, (plane, plane), 0)
    earlier = (lax.broadcasted_iota(jnp.int32, (plane, plane), 1) < row).astype(f32)
    taken = jnp.zeros((plane, places), f32)
    mixing = jnp.zeros((plane, places), f32)
    for j in range(RING):
        named = ids == column_ref[j].astype(f32)
        hit = jnp.max(jnp.where(named, 1.0, 0.0), axis=1, keepdims=True)
        weight = jnp.sum(jnp.where(named, gate, 0.0), axis=1, keepdims=True)
        rank = jnp.dot(
            earlier, jnp.broadcast_to(hit, (plane, NOTE)), preferred_element_type=f32
        )[:, :1]
        mark = (lane == rank.astype(jnp.int32) + j * capacity) & (lane >= j * capacity)
        mark = mark & (lane < (j + 1) * capacity) & (hit > 0.5)
        taken = jnp.where(mark, 1.0, taken)
        mixing = jnp.where(mark, weight, mixing)
    mixing_ref[...] = mixing
    taken = taken.astype(jnp.bfloat16)
    for low in range(0, width, chunk):
        held = jnp.concatenate([b[:, low : low + chunk] for b in blocks], axis=0)
        chosen = lax.dot_general(
            taken, held, (((0,), (0,)), ((), ())), preferred_element_type=f32
        ).astype(jnp.bfloat16)
        for n, chosen_ref in enumerate(chosen_refs):
            chosen_ref[:, low : low + chunk] = chosen[n * capacity : (n + 1) * capacity]


def whole(kernel, out_shape, work, *operands, scalars=()):
    return pl.pallas_call(
        kernel,
        out_shape=out_shape,
        in_specs=[pl.BlockSpec(memory_space=pltpu.SMEM)] * len(scalars)
        + [pl.BlockSpec(memory_space=pltpu.VMEM)] * len(operands),
        out_specs=jax.tree.map(lambda _: pl.BlockSpec(memory_space=pltpu.VMEM), out_shape),
        compiler_params=pltpu.CompilerParams(vmem_limit_bytes=48 << 20),
        cost_estimate=pl.CostEstimate(flops=work, bytes_accessed=1 << 20, transcendentals=0),
    )(*scalars, *operands)


def stack_kernel(*refs):
    low = 0
    for ref in refs[:-1]:
        refs[-1][low : low + ref.shape[0]] = ref[...]
        low += ref.shape[0]


def gated_kernel(chunk, mixing_ref, *refs):
    blocks, (own_ref, *part_refs) = refs[:RING], refs[RING:]
    pieces, rest = [], mixing_ref[...]
    for _ in range(3):
        piece = rest.astype(jnp.bfloat16)
        pieces.append(piece)
        rest = rest - piece.astype(jnp.float32)
    line = own_ref.shape[0]
    for low in range(0, own_ref.shape[1], chunk):
        span = slice(low, low + chunk)
        back = jnp.concatenate([b[:, span] for b in blocks], axis=0)
        total = jnp.dot(pieces[0], back, preferred_element_type=jnp.float32)
        for piece in pieces[1:]:
            total = total + jnp.dot(piece, back, preferred_element_type=jnp.float32)
        own_ref[:, span] = total[:line]
        for n, part_ref in enumerate(part_refs):
            low_row = (n + 1) * line
            part_ref[:, span] = total[low_row : low_row + line].astype(jnp.bfloat16)


def sum_kernel(own_ref, *refs):
    total = own_ref[...]
    for ref in refs[: RING - 1]:
        total = total + ref[...].astype(jnp.float32)
    low = 0
    for ref in refs[RING - 1 :]:
        ref[...] = total[low : low + ref.shape[0]].astype(ref.dtype)
        low += ref.shape[0]


def expert_kernel(chunk, *refs):
    f32 = jnp.float32
    blocks, weights, outs = refs[:RING], refs[RING : RING + 6], refs[RING + 6 :]
    rows = jnp.concatenate([b[...] for b in blocks], axis=0)
    hidden = []
    for gate_ref, up_ref in (weights[:2], weights[3:5]):
        gate_act = jnp.dot(rows, gate_ref[0], preferred_element_type=f32)
        up_act = jnp.dot(rows, up_ref[0], preferred_element_type=f32)
        hidden.append((gate_act / (1.0 + jnp.exp(-gate_act)) * up_act).astype(jnp.bfloat16))
    height = outs[0].shape[0]
    for low in range(0, outs[0].shape[1], chunk):
        span = slice(low, low + chunk)
        total = 0.0
        for part, down_ref in zip(hidden, (weights[2], weights[5])):
            total = total + lax.dot_general(
                part, down_ref[0, span], (((1,), (1,)), ((), ())), preferred_element_type=f32
            )
        for n, out_ref in enumerate(outs):
            out_ref[:, span] = total[n * height : (n + 1) * height].astype(out_ref.dtype)


def pick_kernel(source_ref, from_ref, to_ref, held, came, went):
    count = held.shape[0]
    inward = [
        pltpu.make_async_copy(from_ref.at[source_ref[n]], held.at[n], came.at[n])
        for n in range(count)
    ]
    outward = [pltpu.make_async_copy(held.at[n], to_ref.at[n], went.at[n]) for n in range(count)]
    for copy in inward:
        copy.start()
    for first, second in zip(inward, outward):
        first.wait()
        second.start()
    for copy in outward:
        copy.wait()


def picked(copy_source, spread):
    count = spread.shape[0]
    return pl.pallas_call(
        pick_kernel,
        out_shape=jax.ShapeDtypeStruct(spread.shape, spread.dtype),
        in_specs=[pl.BlockSpec(memory_space=pltpu.SMEM), pl.BlockSpec(memory_space=pl.ANY)],
        out_specs=pl.BlockSpec(memory_space=pl.ANY),
        scratch_shapes=[
            pltpu.VMEM(spread.shape, spread.dtype),
            pltpu.SemaphoreType.DMA((count,)),
            pltpu.SemaphoreType.DMA((count,)),
        ],
        compiler_params=pltpu.CompilerParams(vmem_limit_bytes=16 << 20),
        cost_estimate=pl.CostEstimate(flops=0, bytes_accessed=1 << 20, transcendentals=0),
    )(copy_source, spread)


def copy_kernel(from_ref, to_ref, held, came, went):
    share = held.shape[1]
    spans = [pl.ds(n * share, share) for n in range(held.shape[0])]
    inward = [
        pltpu.make_async_copy(from_ref.at[0, span], held.at[n], came.at[n])
        for n, span in enumerate(spans)
    ]
    outward = [
        pltpu.make_async_copy(held.at[n], to_ref.at[0, span], went.at[n])
        for n, span in enumerate(spans)
    ]
    for copy in inward:
        copy.start()
    for first, second in zip(inward, outward):
        first.wait()
        second.start()
    for copy in outward:
        copy.wait()


def copied(value):
    parts, (_, depth, units) = 8, value.shape
    return pl.pallas_call(
        copy_kernel,
        out_shape=jax.ShapeDtypeStruct(value.shape, value.dtype),
        in_specs=[pl.BlockSpec(memory_space=pl.ANY)],
        out_specs=pl.BlockSpec(memory_space=pl.ANY),
        scratch_shapes=[
            pltpu.VMEM((parts, depth // parts, units), value.dtype),
            pltpu.SemaphoreType.DMA((parts,)),
            pltpu.SemaphoreType.DMA((parts,)),
        ],
        compiler_params=pltpu.CompilerParams(vmem_limit_bytes=16 << 20),
        cost_estimate=pl.CostEstimate(flops=0, bytes_accessed=8 << 20, transcendentals=0),
    )(value)


def part_kernel(from_ref, one_ref, two_ref, held, came, went):
    count, height = held.shape[0], held.shape[1] // 2
    inward = [pltpu.make_async_copy(from_ref.at[n], held.at[n], came.at[n]) for n in range(count)]
    outward = [
        [
            pltpu.make_async_copy(
                held.at[n, pl.ds(k * height, height)],
                to_ref.at[0, pl.ds(n * height, height)],
                went.at[k, n],
            )
            for k, to_ref in enumerate((one_ref, two_ref))
        ]
        for n in range(count)
    ]
    for copy in inward:
        copy.start()
    for first, copies in zip(inward, outward):
        first.wait()
        for copy in copies:
            copy.start()
    for copies in outward:
        for copy in copies:
            copy.wait()


def parted(both):
    count, height, units = both.shape
    out = jax.ShapeDtypeStruct((1, count * height // 2, units), both.dtype)
    return pl.pallas_call(
        part_kernel,
        out_shape=(out, out),
        in_specs=[pl.BlockSpec(memory_space=pl.ANY)],
        out_specs=(pl.BlockSpec(memory_space=pl.ANY),) * 2,
        scratch_shapes=[
            pltpu.VMEM(both.shape, both.dtype),
            pltpu.SemaphoreType.DMA((count,)),
            pltpu.SemaphoreType.DMA((2, count)),
        ],
        compiler_params=pltpu.CompilerParams(vmem_limit_bytes=16 << 20),
        cost_estimate=pl.CostEstimate(flops=0, bytes_accessed=1 << 10, transcendentals=0),
    )(both)


def on_device(tokens, gates, top_ids, home_expert, copy_source, home_gate, home_up, home_down):
    experts = lax.axis_size("expert")
    rows, width = tokens.shape
    fanout = top_ids.shape[1]
    most = (rows * fanout + experts - 1) // experts + 1
    capacity = 4 * RING * most
    depth, units = home_gate.shape[1:]
    blocked = (experts, depth // experts, units)
    here = lax.axis_index("expert")
    core = lax.axis_index("attn") % 2
    z, y, x_hi = here // (2 * RING), here // 2 % RING, here % 2
    bf16, f32 = jnp.bfloat16, jnp.float32
    ahead = jnp.arange(RING, dtype=jnp.int32)
    column = ((z + ahead * (1 - core)) % RING * RING + (y + ahead * core) % RING) * 2 + x_hi
    column_expert = home_expert[column]
    tie = lax.optimization_barrier

    note = jnp.concatenate([top_ids.astype(bf16)] + bf16_pieces(gates), axis=1)
    note = jnp.pad(note, ((0, 0), (0, NOTE - note.shape[1])))
    held, gate_blocks = tie((jnp.concatenate([tokens, note], axis=1), home_gate.reshape(blocked)))
    near = [send(held, row_step(n)) for n in range(1, RING)]
    gate_spread = swap_blocks(gate_blocks)
    both = jnp.concatenate([home_up.reshape(blocked), home_down.reshape(blocked)], axis=1)
    near, far_gate = tie((near, send(home_gate, CORE_SWAP)))
    line = RING * rows
    held = whole(
        stack_kernel, jax.ShapeDtypeStruct((line, width + NOTE), bf16), WORK, held, *near
    )

    blocks = [held] + [send(held, wide_step(n)) for n in range(1, RING)]
    far = (send(home_up, CORE_SWAP), send(home_down, CORE_SWAP))
    blocks, far = tie((blocks, far))
    places = RING * capacity
    *chosen, mixing = whole(
        functools.partial(select_kernel, fanout, capacity, width // 8),
        (jax.ShapeDtypeStruct((capacity, width), bf16),) * RING
        + (jax.ShapeDtypeStruct((RING * line, places), f32),),
        WORK,
        *blocks,
        scalars=(column_expert,),
    )

    both, gate_spread, mixing = tie((both, gate_spread, mixing))
    both_spread = swap_blocks(both)

    mine = [chosen[0]] + [send(chosen[n], deep_step(n)) for n in range(1, RING)]
    summed = whole(
        functools.partial(expert_kernel, width // 8),
        (jax.ShapeDtypeStruct((capacity, width), bf16),) * RING,
        WORK,
        *mine,
        home_gate,
        home_up,
        home_down,
        far_gate,
        *far,
    )
    gate_picks = gate_spread[copy_source]
    gate_picks, both_spread, _ = tie((gate_picks, both_spread, summed[0]))
    replica_gate = swap_blocks(gate_picks)

    back = [summed[0]] + [send(summed[n], deep_step(-n)) for n in range(1, RING)]
    own, *parts = whole(
        functools.partial(gated_kernel, width // 8),
        (jax.ShapeDtypeStruct((line, width), f32),)
        + (jax.ShapeDtypeStruct((line, width), bf16),) * (RING - 1),
        WORK,
        mixing,
        *back,
    )
    parts = [send(parts[n - 1], wide_step(-n)) for n in range(1, RING)]
    both_spread, own = tie((both_spread, own))
    own, both_picks = tie((own, picked(copy_source, both_spread)))
    own, *parts = whole(
        sum_kernel,
        (jax.ShapeDtypeStruct((rows, width), f32),)
        + (jax.ShapeDtypeStruct((rows, width), bf16),) * 3,
        1 << 20,
        own,
        *parts,
    )

    both_picks, replica_gate, own = tie((both_picks, replica_gate, own))
    replica_both = swap_blocks(both_picks)
    replica_gate = copied(replica_gate.reshape(1, depth, units))
    own, replica_gate = tie((own, replica_gate))
    parts = [send(parts[n - 1], row_step(n)) for n in range(1, RING)]
    replica_up, replica_down = parted(replica_both)
    mixed = whole(sum_kernel, (jax.ShapeDtypeStruct((rows, width), bf16),), 1 << 20, own, *parts)[0]
    return (mixed, replica_gate, replica_up, replica_down)


def solution(mesh):
    row_spec = P(("attn", "expert"), None)
    weight_spec = P("expert", None, "attn")
    return jax.shard_map(
        on_device,
        mesh=mesh,
        in_specs=(row_spec, row_spec, row_spec, P(), P(), weight_spec, weight_spec, weight_spec),
        out_specs=(row_spec, weight_spec, weight_spec, weight_spec),
        check_vma=False,
    )
```
